32 devices in a mesh: expert: 16 (over z, y, core), dp: 2 (over x).
Axes of the slice: x: 2, y: 2, z: 4, core: 2. Of those that a mesh axis runs over, the one named last changes fastest.
Arguments:
- tokens: bfloat16 [256, 196, 384], P(('expert', 'dp')), may hold values from -6 to 6
- router: bfloat16 [384, 32], replicated, may hold values from -1 to 65
- expert_in: bfloat16 [32, 384, 1536], P('expert'), may hold values from -2.5 to 2.5
- expert_out: bfloat16 [32, 1536, 384], P('expert'), may hold values from -0.15625 to 0.15625
- out_grad: bfloat16 [256, 196, 384], P(('expert', 'dp')), may hold values from -6 to 6
Outputs:
- grad_tokens: bfloat16 [256, 196, 384], P(('expert', 'dp'))
- grad_in: float32 [32, 384, 1536], P('expert', None, 'dp')
- grad_out: float32 [32, 1536, 384], P('expert', 'dp')
- grad_router: float32 [384, 32], replicated
The draws below stay inside these ranges and needn't reach their ends.
All inputs are finite; a program needn't handle non-finite values.
Results may differ from the reference program's by a relative error of at most 0.017.
Values may be sent and summed in bfloat16 or wider, within the bound.
A program may use at most 64 MiB of HBM per device.

```python
import jax
import jax.numpy as jnp
from jax import lax

D = 384
FF = 1536
PATCHES = 196
IMG_DEV = 8
EXPERTS = 32
IMAGES = 256


def draw_tokens(key, part):
    keys = jax.random.split(key, 1)
    values = jnp.clip(jax.random.normal(keys[0], (IMAGES, PATCHES, D), jnp.float32), -6.0, 6.0)
    return values.astype(jnp.bfloat16)


def draw_router(key, part):
    values = jnp.clip(jax.random.normal(key, (D, EXPERTS), jnp.float32), -6.0, 6.0) / math_root(D)
    return values.astype(jnp.bfloat16)


def math_root(count):
    return float(count) ** 0.5


def block_levels(rng, extent, cuts, least, largest):
    def one(axis_at, shards_of):
        steps = jax.random.uniform(jax.random.fold_in(jax.random.fold_in(rng, 6), axis_at), (shards_of,), jnp.float32, least / len(cuts), largest / len(cuts))
        return jnp.repeat(jnp.exp(steps), extent[axis_at] // shards_of).reshape((-1,) + (1,) * (len(extent) - axis_at - 1))

    factor_of = one(*cuts[0])
    for cut in cuts[1:]:
        factor_of = factor_of * one(*cut)
    return factor_of


def gaussian(rng, shape, spread, most, shards=(), dtype=jnp.bfloat16):
    array = spread * jax.random.normal(rng, shape, jnp.float32)
    if shards:
        array = array * block_levels(rng, shape, shards, -0.22, 0.18)
    return jnp.clip(array, -most, most).astype(dtype)


def setup_inputs(seed: int = 0) -> dict:
    splits = jax.random.split(jax.random.key(seed), 6)
    tokens = draw_tokens(jax.random.fold_in(splits[5], 71), 0)
    router = draw_router(jax.random.fold_in(splits[5], 71), 0)
    expert_in = gaussian(splits[2], (EXPERTS, D, FF), (D // 64) ** -0.5, 2.5, ((0, 16),))
    expert_out = gaussian(splits[3], (EXPERTS, FF, D), FF ** -0.5, 0.15625, ((0, 16),))
    out_grad = gaussian(splits[4], (IMAGES, PATCHES, D), 1.0, 6.0, ((0, 32),))
    return {"tokens": tokens, "router": router, "expert_in": expert_in, "expert_out": expert_out, "out_grad": out_grad}


def reference(tokens, router, expert_in, expert_out, out_grad):
    router_wide = router.astype(jnp.float32)

    def slot_side(block):
        images, cotangent = block
        logits = jnp.einsum('bpd,ds->bps', images.astype(jnp.float32), router_wide)
        dispatch_low = jax.nn.softmax(logits, axis=1).astype(jnp.bfloat16)
        combine_low = jax.nn.softmax(logits, axis=2).astype(jnp.bfloat16)
        slots = jnp.einsum('bps,bpd->bsd', dispatch_low.astype(jnp.float32), images.astype(jnp.float32)).astype(jnp.bfloat16)
        slot_grads = jnp.einsum('bps,bpd->bsd', combine_low.astype(jnp.float32), cotangent.astype(jnp.float32)).astype(jnp.bfloat16)
        return (slots, slot_grads)
    shaped_tokens = tokens.reshape((-1, IMG_DEV, PATCHES, D))
    shaped_grads = out_grad.reshape((-1, IMG_DEV, PATCHES, D))
    slots, slot_grads = lax.map(slot_side, (shaped_tokens, shaped_grads))
    slots = slots.reshape((IMAGES, EXPERTS, D))
    slot_grads = slot_grads.reshape((IMAGES, EXPERTS, D))

    def expert_side(block):
        inputs, grads, first, second = block
        hidden = jnp.dot(inputs, first, preferred_element_type=jnp.float32)
        activated, gelu_back = jax.vjp(jax.nn.gelu, hidden)
        activated_low = activated.astype(jnp.bfloat16)
        slot_out = jnp.dot(activated_low, second, preferred_element_type=jnp.float32).astype(jnp.bfloat16)
        act_grad = jnp.dot(grads, second.T, preferred_element_type=jnp.float32)
        hidden_grad = gelu_back(act_grad)[0].astype(jnp.bfloat16)
        slot_in_grad = jnp.dot(hidden_grad, first.T, preferred_element_type=jnp.float32).astype(jnp.bfloat16)
        first_grad = jnp.dot(inputs.T, hidden_grad, preferred_element_type=jnp.float32)
        second_grad = jnp.dot(activated_low.T, grads, preferred_element_type=jnp.float32)
        return (slot_out, slot_in_grad, first_grad, second_grad)
    slot_out, slot_in_grad, grad_in, grad_out = lax.map(expert_side, (jnp.moveaxis(slots, 1, 0), jnp.moveaxis(slot_grads, 1, 0), expert_in, expert_out))
    slot_out = jnp.moveaxis(slot_out, 0, 1).reshape((-1, IMG_DEV, EXPERTS, D))
    slot_in_grad = jnp.moveaxis(slot_in_grad, 0, 1).reshape((-1, IMG_DEV, EXPERTS, D))

    def token_side(block):
        images, cotangent, outputs, inputs_grad = block
        images_wide = images.astype(jnp.float32)
        logits = jnp.einsum('bpd,ds->bps', images_wide, router_wide)
        dispatch = jax.nn.softmax(logits, axis=1)
        combine = jax.nn.softmax(logits, axis=2)
        dispatch_low = dispatch.astype(jnp.bfloat16)
        combine_grad = jnp.einsum('bpd,bsd->bps', cotangent.astype(jnp.float32), outputs.astype(jnp.float32))
        dispatch_grad = jnp.einsum('bpd,bsd->bps', images_wide, inputs_grad.astype(jnp.float32))
        logit_grad = dispatch * (dispatch_grad - lax.optimization_barrier(jnp.sum(dispatch * dispatch_grad, axis=1, keepdims=True)))
        logit_grad = logit_grad + combine * (combine_grad - lax.optimization_barrier(jnp.sum(combine * combine_grad, axis=2, keepdims=True)))
        logit_low = logit_grad.astype(jnp.bfloat16).astype(jnp.float32)
        first_part = jnp.einsum('bps,bsd->bpd', dispatch_low.astype(jnp.float32), inputs_grad.astype(jnp.float32))
        second_part = jnp.einsum('bps,ds->bpd', logit_low, router_wide)
        token_grad = (first_part + second_part).astype(jnp.bfloat16)
        router_term = jnp.einsum('bpd,bps->ds', images_wide, logit_low)
        return (token_grad, router_term)
    grad_tokens, router_terms = lax.map(token_side, (shaped_tokens, shaped_grads, slot_out, slot_in_grad))
    grad_tokens = grad_tokens.reshape((IMAGES, PATCHES, D))
    grad_router = lax.optimization_barrier(jnp.sum(router_terms, axis=0))
    return (grad_tokens, grad_in, grad_out, grad_router)
```

```python
import functools

import jax
import jax.numpy as jnp
from jax import lax
from jax.sharding import PartitionSpec as P


def to_experts(x, n):
    wide = lax.all_to_all(x, "expert", split_axis=0, concat_axis=1, tiled=True)
    return wide.reshape(wide.shape[0], n, x.shape[1], x.shape[2])


def to_images(x, n):
    flat = x.reshape(x.shape[0], n * x.shape[2], x.shape[3])
    return lax.all_to_all(flat, "expert", split_axis=1, concat_axis=0, tiled=True)


def sum_all(x, n, dp):
    return lax.psum(x, ("expert", "dp"))


def on_device(n, dp, tokens, router, expert_in, expert_out, out_grad):
    f32, low = jnp.float32, jnp.bfloat16
    dot = functools.partial(jnp.einsum, preferred_element_type=f32)
    images = tokens.shape[0]
    logits = dot("bpd,ds->bps", tokens, router)
    dispatch = jax.nn.softmax(logits, axis=1)
    combine = jax.nn.softmax(logits, axis=2)
    dispatch_low = dispatch.astype(low)
    combine_low = combine.astype(low)
    slots = dot("bps,bpd->sbd", dispatch_low, tokens).astype(low)
    slot_grads = dot("bps,bpd->sbd", combine_low, out_grad).astype(low)
    here = to_experts(jnp.concatenate([slots, slot_grads], axis=1), n)
    each, width = here.shape[0], here.shape[3]
    everyone = lax.all_gather(here, "dp", axis=1, tiled=True)

    def halves(block):
        flat = (each, block.shape[1] * images, width)
        return block[:, :, :images].reshape(flat), block[:, :, images:].reshape(flat)

    def hidden_side(inputs, grads, first, second):
        hidden = dot("jrd,jdf->jrf", inputs, first)
        activated, gelu_back = jax.vjp(jax.nn.gelu, hidden)
        act_grad = dot("jrd,jfd->jrf", grads, second)
        return activated.astype(low), gelu_back(act_grad)[0].astype(low)

    slots_here, grads_here = halves(here)
    activated, hidden_grad = hidden_side(slots_here, grads_here, expert_in, expert_out)
    outputs_here = dot("jrf,jfd->jrd", activated, expert_out).astype(low)
    input_grad_here = dot("jrf,jdf->jrd", hidden_grad, expert_in).astype(low)
    split = (each, n, images, width)
    back = to_images(
        jnp.concatenate([outputs_here.reshape(split), input_grad_here.reshape(split)], axis=2), n
    )
    outputs, inputs_grad = back[:, :images], back[:, images:]

    units = expert_in.shape[2] // dp
    start = lax.axis_index("dp") * units
    first = lax.dynamic_slice_in_dim(expert_in, start, units, axis=2)
    second = lax.dynamic_slice_in_dim(expert_out, start, units, axis=1)
    slots_all, grads_all = halves(everyone)
    activated_all, hidden_grad_all = hidden_side(slots_all, grads_all, first, second)
    grad_in = dot("jrd,jrf->jdf", slots_all, hidden_grad_all)
    grad_out = dot("jrf,jrd->jfd", activated_all, grads_all)

    combine_grad = dot("bpd,sbd->bps", out_grad, outputs)
    dispatch_grad = dot("bpd,sbd->bps", tokens, inputs_grad)
    logit_grad = dispatch * (
        dispatch_grad - jnp.sum(dispatch * dispatch_grad, axis=1, keepdims=True)
    )
    logit_grad = logit_grad + combine * (
        combine_grad - jnp.sum(combine * combine_grad, axis=2, keepdims=True)
    )
    logit_low = logit_grad.astype(low)
    first_part = dot("bps,sbd->bpd", dispatch_low, inputs_grad)
    second_part = dot("bps,ds->bpd", logit_low, router)
    grad_tokens = (first_part + second_part).astype(low)
    router_term = dot("bps,bpd->sd", logit_low, tokens)
    grad_router = sum_all(router_term, n, dp).T
    return (grad_tokens, grad_in, grad_out, grad_router)


def solution(mesh):
    placed = (
        P(("expert", "dp"), None, None),
        P(),
        P("expert", None, None),
        P("expert", None, None),
        P(("expert", "dp"), None, None),
    )
    return jax.shard_map(
        functools.partial(on_device, mesh.shape["expert"], mesh.shape["dp"]),
        mesh=mesh,
        in_specs=placed,
        out_specs=(
            P(("expert", "dp"), None, None),
            P("expert", None, "dp"),
            P("expert", "dp", None),
            P(),
        ),
        check_vma=False,
    )
```

```python
import functools

import jax
import jax.numpy as jnp
from jax import lax
from jax.experimental import pallas as pl
from jax.experimental.pallas import tpu as pltpu
from jax.sharding import PartitionSpec as P

MESH = pl.DeviceIdType.MESH


def greet(n):
    me = lax.axis_index("expert")
    barrier = pltpu.get_barrier_semaphore()

    @pl.loop(1, n)
    def _(k):
        pl.semaphore_signal(
            barrier, inc=1, device_id={"expert": lax.rem(me + k, n)}, device_id_type=MESH
        )

    return me, barrier


def exchange_kernel(n, outward, x_ref, y_ref, send_sem, recv_sem, own_sem):
    me, barrier = greet(n)

    def block(peer):
        return x_ref.at[peer] if outward else x_ref.at[:, peer]

    landing = y_ref.at[:, me] if outward else y_ref.at[me]
    own = pltpu.make_async_copy(block(me), landing, own_sem)
    own.start()
    pl.semaphore_wait(barrier, n - 1)

    def copy(k):
        peer = lax.rem(me + k, n)
        return pltpu.make_async_remote_copy(
            src_ref=block(peer),
            dst_ref=landing,
            send_sem=send_sem.at[k],
            recv_sem=recv_sem.at[k],
            device_id={"expert": peer},
            device_id_type=MESH,
        )

    @pl.loop(1, n)
    def _(k):
        copy(k).start()

    own.wait()

    @pl.loop(1, n)
    def _(k):
        copy(k).wait()


def exchange(x, n, shape, outward, collective_id):
    return pl.pallas_call(
        functools.partial(exchange_kernel, n, outward),
        out_shape=jax.ShapeDtypeStruct(shape, x.dtype),
        in_specs=[pl.BlockSpec(memory_space=pltpu.VMEM)],
        out_specs=pl.BlockSpec(memory_space=pltpu.VMEM),
        scratch_shapes=[
            pltpu.SemaphoreType.DMA((n,)),
            pltpu.SemaphoreType.DMA((n,)),
            pltpu.SemaphoreType.DMA,
        ],
        compiler_params=pltpu.CompilerParams(
            collective_id=collective_id, has_side_effects=True
        ),
    )(x)


def to_experts(x, n):
    each = x.shape[0] // n
    x = x.reshape(n, each, x.shape[1], x.shape[2])
    return exchange(x, n, (each, n, x.shape[2], x.shape[3]), True, 0)


def to_images(x, n):
    y = exchange(x, n, (n, x.shape[0], x.shape[2], x.shape[3]), False, 1)
    return y.reshape(n * x.shape[0], x.shape[2], x.shape[3])


def sum_kernel(n, dp, x_ref, y_ref, terms, halves, total, send_a, recv_a, send_b, recv_b, send_c, recv_c):
    me, barrier = greet(n)
    row = lax.axis_index("dp")

    @pl.loop(1, dp)
    def _(k):
        pl.semaphore_signal(
            barrier, inc=1, device_id={"dp": lax.rem(row + k, dp)}, device_id_type=MESH
        )

    pl.semaphore_wait(barrier, n + dp - 2)

    def send(src, dst, sends, recvs, k, axis, place, size):
        return pltpu.make_async_remote_copy(
            src_ref=src,
            dst_ref=dst,
            send_sem=sends.at[k],
            recv_sem=recvs.at[k],
            device_id={axis: lax.rem(place + k, size)},
            device_id_type=MESH,
        )

    def first(k):
        return send(x_ref.at[lax.rem(me + k, n)], terms.at[me], send_a, recv_a, k, "expert", me, n)

    def second(k):
        return send(halves.at[row], halves.at[row], send_b, recv_b, k, "dp", row, dp)

    def third(k):
        return send(total, y_ref.at[me], send_c, recv_c, k, "expert", me, n)

    def run(copy, size):
        @pl.loop(1, size)
        def _(k):
            copy(k).start()

        @pl.loop(1, size)
        def _(k):
            copy(k).wait()

    terms[me] = x_ref[me]
    run(first, n)
    halves[row] = jnp.sum(terms[...], axis=0)
    run(second, dp)
    total[...] = jnp.sum(halves[...], axis=0)
    y_ref[me] = total[...]
    run(third, n)


def sum_all(x, n, dp):
    each = x.shape[0] // n
    block = (each, x.shape[1])
    y = pl.pallas_call(
        functools.partial(sum_kernel, n, dp),
        out_shape=jax.ShapeDtypeStruct((n,) + block, x.dtype),
        in_specs=[pl.BlockSpec(memory_space=pltpu.VMEM)],
        out_specs=pl.BlockSpec(memory_space=pltpu.VMEM),
        scratch_shapes=[
            pltpu.VMEM((n,) + block, x.dtype),
            pltpu.VMEM((dp,) + block, x.dtype),
            pltpu.VMEM(block, x.dtype),
            pltpu.SemaphoreType.DMA((n,)),
            pltpu.SemaphoreType.DMA((n,)),
            pltpu.SemaphoreType.DMA((dp,)),
            pltpu.SemaphoreType.DMA((dp,)),
            pltpu.SemaphoreType.DMA((n,)),
            pltpu.SemaphoreType.DMA((n,)),
        ],
        compiler_params=pltpu.CompilerParams(collective_id=2, has_side_effects=True),
    )(x.reshape((n,) + block))
    return y.reshape(x.shape)


def on_device(n, dp, tokens, router, expert_in, expert_out, out_grad):
    f32, low = jnp.float32, jnp.bfloat16
    dot = functools.partial(jnp.einsum, preferred_element_type=f32)
    images = tokens.shape[0]
    logits = dot("bpd,ds->bps", tokens, router)
    dispatch = jax.nn.softmax(logits, axis=1)
    combine = jax.nn.softmax(logits, axis=2)
    dispatch_low = dispatch.astype(low)
    combine_low = combine.astype(low)
    slots = dot("bps,bpd->sbd", dispatch_low, tokens).astype(low)
    slot_grads = dot("bps,bpd->sbd", combine_low, out_grad).astype(low)
    here = to_experts(jnp.concatenate([slots, slot_grads], axis=1), n)
    each, width = here.shape[0], here.shape[3]
    everyone = lax.all_gather(here, "dp", axis=1, tiled=True)

    def halves(block):
        flat = (each, block.shape[1] * images, width)
        return block[:, :, :images].reshape(flat), block[:, :, images:].reshape(flat)

    def hidden_side(inputs, grads, first, second):
        hidden = dot("jrd,jdf->jrf", inputs, first)
        activated, gelu_back = jax.vjp(jax.nn.gelu, hidden)
        act_grad = dot("jrd,jfd->jrf", grads, second)
        return activated.astype(low), gelu_back(act_grad)[0].astype(low)

    slots_here, grads_here = halves(here)
    activated, hidden_grad = hidden_side(slots_here, grads_here, expert_in, expert_out)
    outputs_here = dot("jrf,jfd->jrd", activated, expert_out).astype(low)
    input_grad_here = dot("jrf,jdf->jrd", hidden_grad, expert_in).astype(low)
    split = (each, n, images, width)
    back = to_images(
        jnp.concatenate([outputs_here.reshape(split), input_grad_here.reshape(split)], axis=2), n
    )
    outputs, inputs_grad = back[:, :images], back[:, images:]

    units = expert_in.shape[2] // dp
    start = lax.axis_index("dp") * units
    first = lax.dynamic_slice_in_dim(expert_in, start, units, axis=2)
    second = lax.dynamic_slice_in_dim(expert_out, start, units, axis=1)
    slots_all, grads_all = halves(everyone)
    activated_all, hidden_grad_all = hidden_side(slots_all, grads_all, first, second)
    grad_in = dot("jrd,jrf->jdf", slots_all, hidden_grad_all)
    grad_out = dot("jrf,jrd->jfd", activated_all, grads_all)

    combine_grad = dot("bpd,sbd->bps", out_grad, outputs)
    dispatch_grad = dot("bpd,sbd->bps", tokens, inputs_grad)
    logit_grad = dispatch * (
        dispatch_grad - jnp.sum(dispatch * dispatch_grad, axis=1, keepdims=True)
    )
    logit_grad = logit_grad + combine * (
        combine_grad - jnp.sum(combine * combine_grad, axis=2, keepdims=True)
    )
    logit_low = logit_grad.astype(low)
    first_part = dot("bps,sbd->bpd", dispatch_low, inputs_grad)
    second_part = dot("bps,ds->bpd", logit_low, router)
    grad_tokens = (first_part + second_part).astype(low)
    router_term = dot("bps,bpd->sd", logit_low, tokens)
    grad_router = sum_all(router_term, n, dp).T
    return (grad_tokens, grad_in, grad_out, grad_router)


def solution(mesh):
    placed = (
        P(("expert", "dp"), None, None),
        P(),
        P("expert", None, None),
        P("expert", None, None),
        P(("expert", "dp"), None, None),
    )
    return jax.shard_map(
        functools.partial(on_device, mesh.shape["expert"], mesh.shape["dp"]),
        mesh=mesh,
        in_specs=placed,
        out_specs=(
            P(("expert", "dp"), None, None),
            P("expert", None, "dp"),
            P("expert", "dp", None),
            P(),
        ),
        check_vma=False,
    )
```

```python
import functools

import jax
import jax.numpy as jnp
from jax import lax
from jax.experimental import pallas as pl
from jax.experimental.pallas import tpu as pltpu
from jax.sharding import PartitionSpec as P

MESH = pl.DeviceIdType.MESH


def greet(n):
    me = lax.axis_index("expert")
    barrier = pltpu.get_barrier_semaphore()

    @pl.loop(1, n)
    def _(k):
        pl.semaphore_signal(
            barrier, inc=1, device_id={"expert": lax.rem(me + k, n)}, device_id_type=MESH
        )

    return me, barrier


def greet_dp(dp, barrier):
    row = lax.axis_index("dp")

    @pl.loop(1, dp)
    def _(k):
        pl.semaphore_signal(
            barrier, inc=1, device_id={"dp": lax.rem(row + k, dp)}, device_id_type=MESH
        )

    return row


def exchange_kernel(n, outward, x_ref, y_ref, send_sem, recv_sem, own_sem):
    me, barrier = greet(n)

    def block(peer):
        return x_ref.at[peer] if outward else x_ref.at[:, peer]

    landing = y_ref.at[:, me] if outward else y_ref.at[me]
    own = pltpu.make_async_copy(block(me), landing, own_sem)
    own.start()
    pl.semaphore_wait(barrier, n - 1)

    def copy(k):
        peer = lax.rem(me + k, n)
        return pltpu.make_async_remote_copy(
            src_ref=block(peer),
            dst_ref=landing,
            send_sem=send_sem.at[k],
            recv_sem=recv_sem.at[k],
            device_id={"expert": peer},
            device_id_type=MESH,
        )

    @pl.loop(1, n)
    def _(k):
        copy(k).start()

    own.wait()

    @pl.loop(1, n)
    def _(k):
        copy(k).wait()


def exchange(x, n, shape, outward, collective_id):
    return pl.pallas_call(
        functools.partial(exchange_kernel, n, outward),
        out_shape=jax.ShapeDtypeStruct(shape, x.dtype),
        in_specs=[pl.BlockSpec(memory_space=pltpu.VMEM)],
        out_specs=pl.BlockSpec(memory_space=pltpu.VMEM),
        scratch_shapes=[
            pltpu.SemaphoreType.DMA((n,)),
            pltpu.SemaphoreType.DMA((n,)),
            pltpu.SemaphoreType.DMA,
        ],
        compiler_params=pltpu.CompilerParams(
            collective_id=collective_id, has_side_effects=True
        ),
    )(x)


def to_experts(x, n):
    each = x.shape[0] // n
    x = x.reshape(n, each, x.shape[1], x.shape[2])
    return exchange(x, n, (each, n, x.shape[2], x.shape[3]), True, 0)


def back_kernel(n, dp, x_ref, here_ref, y_ref, all_ref, send_sem, recv_sem, send_dp, recv_dp, own_sem):
    me, barrier = greet(n)
    row = greet_dp(dp, barrier)
    place = all_ref.at[:, pl.ds(row * n, n)]
    keep = pltpu.make_async_copy(here_ref, place, own_sem.at[0])
    own = pltpu.make_async_copy(x_ref.at[:, me], y_ref.at[me], own_sem.at[1])
    keep.start()
    own.start()
    pl.semaphore_wait(barrier, n + dp - 2)

    def copy(k):
        peer = lax.rem(me + k, n)
        return pltpu.make_async_remote_copy(
            src_ref=x_ref.at[:, peer],
            dst_ref=y_ref.at[me],
            send_sem=send_sem.at[k],
            recv_sem=recv_sem.at[k],
            device_id={"expert": peer},
            device_id_type=MESH,
        )

    def across(k):
        return pltpu.make_async_remote_copy(
            src_ref=here_ref,
            dst_ref=place,
            send_sem=send_dp.at[k],
            recv_sem=recv_dp.at[k],
            device_id={"dp": lax.rem(row + k, dp)},
            device_id_type=MESH,
        )

    @pl.loop(1, dp)
    def _(k):
        across(k).start()

    @pl.loop(1, n)
    def _(k):
        copy(k).start()

    keep.wait()
    own.wait()

    @pl.loop(1, n)
    def _(k):
        copy(k).wait()

    @pl.loop(1, dp)
    def _(k):
        across(k).wait()


def to_images(x, here, n, dp):
    each, _, rows, width = x.shape
    y, everyone = pl.pallas_call(
        functools.partial(back_kernel, n, dp),
        out_shape=(
            jax.ShapeDtypeStruct((n, each, rows, width), x.dtype),
            jax.ShapeDtypeStruct((each, dp * n, rows, width), x.dtype),
        ),
        in_specs=[pl.BlockSpec(memory_space=pltpu.VMEM)] * 2,
        out_specs=(pl.BlockSpec(memory_space=pltpu.VMEM),) * 2,
        scratch_shapes=[
            pltpu.SemaphoreType.DMA((n,)),
            pltpu.SemaphoreType.DMA((n,)),
            pltpu.SemaphoreType.DMA((dp,)),
            pltpu.SemaphoreType.DMA((dp,)),
            pltpu.SemaphoreType.DMA((2,)),
        ],
        compiler_params=pltpu.CompilerParams(
            collective_id=1, has_side_effects=True, vmem_limit_bytes=24 * 1024 * 1024
        ),
    )(x, here)
    return y.reshape(n * each, rows, width), everyone


def sum_kernel(n, dp, x_ref, y_ref, terms, halves, total, send_a, recv_a, send_b, recv_b, send_c, recv_c):
    me, barrier = greet(n)
    row = greet_dp(dp, barrier)
    pl.semaphore_wait(barrier, n + dp - 2)

    def send(src, dst, sends, recvs, k, axis, place, size):
        return pltpu.make_async_remote_copy(
            src_ref=src,
            dst_ref=dst,
            send_sem=sends.at[k],
            recv_sem=recvs.at[k],
            device_id={axis: lax.rem(place + k, size)},
            device_id_type=MESH,
        )

    def first(k):
        return send(x_ref.at[lax.rem(me + k, n)], terms.at[me], send_a, recv_a, k, "expert", me, n)

    def second(k):
        return send(halves.at[row], halves.at[row], send_b, recv_b, k, "dp", row, dp)

    def third(k):
        return send(total, y_ref.at[me], send_c, recv_c, k, "expert", me, n)

    def run(copy, size):
        @pl.loop(1, size)
        def _(k):
            copy(k).start()

        @pl.loop(1, size)
        def _(k):
            copy(k).wait()

    terms[me] = x_ref[me]
    run(first, n)
    halves[row] = jnp.sum(terms[...], axis=0)
    run(second, dp)
    total[...] = jnp.sum(halves[...], axis=0)
    y_ref[me] = total[...]
    run(third, n)


def sum_all(x, n, dp):
    each = x.shape[0] // n
    block = (each, x.shape[1])
    y = pl.pallas_call(
        functools.partial(sum_kernel, n, dp),
        out_shape=jax.ShapeDtypeStruct((n,) + block, x.dtype),
        in_specs=[pl.BlockSpec(memory_space=pltpu.VMEM)],
        out_specs=pl.BlockSpec(memory_space=pltpu.VMEM),
        scratch_shapes=[
            pltpu.VMEM((n,) + block, x.dtype),
            pltpu.VMEM((dp,) + block, x.dtype),
            pltpu.VMEM(block, x.dtype),
            pltpu.SemaphoreType.DMA((n,)),
            pltpu.SemaphoreType.DMA((n,)),
            pltpu.SemaphoreType.DMA((dp,)),
            pltpu.SemaphoreType.DMA((dp,)),
            pltpu.SemaphoreType.DMA((n,)),
            pltpu.SemaphoreType.DMA((n,)),
        ],
        compiler_params=pltpu.CompilerParams(collective_id=2, has_side_effects=True),
    )(x.reshape((n,) + block))
    return y.reshape(x.shape)


def on_device(n, dp, tokens, router, expert_in, expert_out, out_grad):
    f32, low = jnp.float32, jnp.bfloat16
    dot = functools.partial(jnp.einsum, preferred_element_type=f32)
    images = tokens.shape[0]
    logits = dot("bpd,ds->bps", tokens, router)
    dispatch = jax.nn.softmax(logits, axis=1)
    combine = jax.nn.softmax(logits, axis=2)
    dispatch_low = dispatch.astype(low)
    combine_low = combine.astype(low)
    slots = dot("bps,bpd->sbd", dispatch_low, tokens).astype(low)
    slot_grads = dot("bps,bpd->sbd", combine_low, out_grad).astype(low)
    here = to_experts(jnp.concatenate([slots, slot_grads], axis=1), n)
    each, width = here.shape[0], here.shape[3]

    def halves(block):
        flat = (each, block.shape[1] * images, width)
        return block[:, :, :images].reshape(flat), block[:, :, images:].reshape(flat)

    def hidden_side(inputs, grads, first, second):
        hidden = dot("jrd,jdf->jrf", inputs, first)
        activated, gelu_back = jax.vjp(jax.nn.gelu, hidden)
        act_grad = dot("jrd,jfd->jrf", grads, second)
        return activated.astype(low), gelu_back(act_grad)[0].astype(low)

    slots_here, grads_here = halves(here)
    activated, hidden_grad = hidden_side(slots_here, grads_here, expert_in, expert_out)
    outputs_here = dot("jrf,jfd->jrd", activated, expert_out).astype(low)
    input_grad_here = dot("jrf,jdf->jrd", hidden_grad, expert_in).astype(low)
    split = (each, n, images, width)
    back, everyone = to_images(
        jnp.concatenate([outputs_here.reshape(split), input_grad_here.reshape(split)], axis=2),
        here,
        n,
        dp,
    )
    outputs, inputs_grad = back[:, :images], back[:, images:]

    units = expert_in.shape[2] // dp
    start = lax.axis_index("dp") * units
    first = lax.dynamic_slice_in_dim(expert_in, start, units, axis=2)
    second = lax.dynamic_slice_in_dim(expert_out, start, units, axis=1)
    slots_all, grads_all = halves(everyone)
    activated_all, hidden_grad_all = hidden_side(slots_all, grads_all, first, second)
    grad_in = dot("jrd,jrf->jdf", slots_all, hidden_grad_all)
    grad_out = dot("jrf,jrd->jfd", activated_all, grads_all)

    combine_grad = dot("bpd,sbd->bps", out_grad, outputs)
    dispatch_grad = dot("bpd,sbd->bps", tokens, inputs_grad)
    logit_grad = dispatch * (
        dispatch_grad - jnp.sum(dispatch * dispatch_grad, axis=1, keepdims=True)
    )
    logit_grad = logit_grad + combine * (
        combine_grad - jnp.sum(combine * combine_grad, axis=2, keepdims=True)
    )
    logit_low = logit_grad.astype(low)
    first_part = dot("bps,sbd->bpd", dispatch_low, inputs_grad)
    second_part = dot("bps,ds->bpd", logit_low, router)
    grad_tokens = (first_part + second_part).astype(low)
    router_term = dot("bps,bpd->sd", logit_low, tokens)
    grad_router = sum_all(router_term, n, dp).T
    return (grad_tokens, grad_in, grad_out, grad_router)


def solution(mesh):
    placed = (
        P(("expert", "dp"), None, None),
        P(),
        P("expert", None, None),
        P("expert", None, None),
        P(("expert", "dp"), None, None),
    )
    return jax.shard_map(
        functools.partial(on_device, mesh.shape["expert"], mesh.shape["dp"]),
        mesh=mesh,
        in_specs=placed,
        out_specs=(
            P(("expert", "dp"), None, None),
            P("expert", None, "dp"),
            P("expert", "dp", None),
            P(),
        ),
        check_vma=False,
    )
```
